256 devices in a mesh: len: 64 (over z, y, core), sec: 4 (over x).
Axes of the slice: x: 4, y: 4, z: 8, core: 2. Of those that a mesh axis runs over, the one named last changes fastest.
Arguments:
- predicted: float32 [3, 1024, 128, 128], P(None, 'len', 'sec'), may hold values from -6 to 6
- material: int32 [1024, 128, 128], P('len', 'sec'), may hold values from 0 to 7
- stiffness_table: float32 [8], replicated, may hold values from 1 to 10
- density_table: float32 [8], replicated, may hold values from 0.5 to 2
- contact_tile: int32 [4096, 1], P('len'), may hold values from 0 to 63; in each aligned block of 64 rows (0 to 63, 64 to 127, ...) at most 2 rows name the same one
- contact_row: int32 [4096], P('len'), may hold values from 0 to 2047
- contact_force: float32 [4096, 3, 128], P('len'), may hold values from -6 to 6
Outputs:
- displacement: float32 [3, 1024, 128, 128], P(None, 'len', 'sec')
- residual: float32 [3, 1024, 128, 128], P(None, 'len', 'sec')
The draws below stay inside these ranges and needn't reach their ends.
Inputs may be any that keep to these rules, and one draw needn't show every extreme that they name: `contact_tile`: within the 64 rows of each index of len, no tile is named more than 2 times, a bound that some block reaches.
All inputs are finite; a program needn't handle non-finite values.
Results may differ from the reference program's by a relative error of at most 0.0003.
Values sent between devices are 32-bit elements; how exact they have to be, the bound alone decides.
A program may use at most 64 MiB of HBM per device.

```python
import math
import jax
import jax.numpy as jnp
import numpy as np
from jax import lax

CX = 16
NZ = 128
CONT_DEV = 64
NMAT = 8
CAP = 2
CONTACTS = 4096
NX = 1024
NY = 128
N_LEN = 64


def with_ends(array, stream_key, smallest, largest):
    dims = array.shape
    spot = [jax.random.randint(jax.random.fold_in(stream_key, axis), (), 0, dims[axis]) for axis in range(len(dims))]
    array = array.at[tuple(spot)].set(smallest)
    longest = dims.index(max(dims))
    spot[longest] = (spot[longest] + 1) % dims[longest]
    return array.at[tuple(spot)].set(largest)


def level_of(own_key, dims, cuts, least, largest):
    def one(position, shards_of):
        heights = jax.random.uniform(jax.random.fold_in(jax.random.fold_in(own_key, 6), position), (shards_of,), jnp.float32, least / len(cuts), largest / len(cuts))
        return jnp.repeat(jnp.exp(heights), dims[position] // shards_of).reshape((-1,) + (1,) * (len(dims) - position - 1))

    gain = one(*cuts[0])
    for cut in cuts[1:]:
        gain = gain * one(*cut)
    return gain


def shared_out(own_key, own, number, rows, count, top, limit, skew):
    ranking = jax.random.permutation(own_key, count)
    packed, usual = portions_of(count, rows * top, limit, skew, True), portions_of(count, rows * top, limit, skew, False)
    places = jnp.arange(count)

    def named(sizes, offset_by):
        used = int((sizes > 0).sum())
        fixed = max(1, used // 4)
        moved = fixed + (places - fixed + offset_by * (used - fixed)) % max(1, count - fixed)
        return jnp.zeros((count,), jnp.int32).at[ranking[jnp.where(places < fixed, places, moved)]].set(jnp.asarray(sizes, jnp.int32))

    sizes = jnp.where(number % 4 == 0, named(packed, number // 4), named(usual, number - number // 4 - 1))
    mixed = jax.random.permutation(jax.random.fold_in(own, 3), count)
    giver, receiver = mixed[0:count // 2 * 2:2], mixed[1:count // 2 * 2:2]
    room = jnp.minimum(sizes[giver] - 1, limit - sizes[receiver]) // 2
    room = jnp.where((giver == ranking[0]) | (receiver == ranking[0]) | (sizes[receiver] == 0), 0, jnp.maximum(room, 0))
    moved = jax.random.randint(jax.random.fold_in(own, 4), (count // 2,), 0, 1 << 20) % (room + 1)
    sizes = sizes.at[giver].add(-moved).at[receiver].add(moved)
    labels = jnp.searchsorted(jnp.cumsum(sizes), jnp.arange(rows * top), side="right").astype(jnp.int32)
    listing = labels.reshape(top, rows).T
    listing = listing[jax.random.permutation(jax.random.fold_in(own, 1), rows)]
    offset_by = jax.random.randint(jax.random.fold_in(own, 2), (rows, 1), 0, top)
    return jnp.take_along_axis(listing, (jnp.arange(top)[None, :] + offset_by) % top, axis=1)


def portions_of(number_of, total, limit, slope, full):
    loads = [(1 << 20) // math.isqrt(standing ** slope) + 1 for standing in range(1, number_of + 1)]
    largest = limit if full else min(limit, max(-(-total // number_of), total * loads[0] // sum(loads)))
    least = 1 if total - largest >= number_of - 1 else 0
    holding, rest = [largest] + [least] * (number_of - 1), total - largest - least * (number_of - 1)
    while rest > 0:
        candidates = [i for i in range(1, number_of) if holding[i] < largest] or [i for i in range(1, number_of) if holding[i] < limit]
        pool, budget = sum([loads[i] for i in candidates]), rest
        for i in candidates:
            addition = min(limit - holding[i], max(1, budget * loads[i] // pool), rest)
            holding[i] = holding[i] + addition
            rest = rest - addition
    return np.array(holding)


def noise(own_key, extent, spread, limit, cuts=(), kind=jnp.bfloat16):
    array = jax.random.normal(own_key, extent, jnp.float32) * spread
    if len(cuts) > 0:
        array = level_of(own_key, extent, cuts, -0.22, 0.18) * array
    return jnp.clip(array, min=-limit, max=limit).astype(kind)


def setup_inputs(seed: int = 0) -> dict:
    keys = jax.random.split(jax.random.key(seed), 8)
    predicted = noise(keys[0], (3, NX, NY, NZ), 1.0, 6.0, ((1, 64), (2, 4)), jnp.float32)
    material = with_ends(jax.random.randint(keys[1], (NX, NY, NZ), 0, NMAT), jax.random.fold_in(keys[1], 1), 0, NMAT - 1).astype(jnp.int32)
    stiffness_table = jnp.clip(jnp.exp(jax.random.uniform(keys[2], (NMAT,), jnp.float32, math.log(1.0), math.log(10.0))), 1.0, 10.0)
    density_table = jnp.clip(jnp.exp(jax.random.uniform(keys[3], (NMAT,), jnp.float32, math.log(0.5), math.log(2.0))), 0.5, 2.0)
    contact_tile_keys = jax.random.split(jax.random.fold_in(keys[4], 1), CONTACTS // CONT_DEV)
    contact_tile_turns = jax.random.permutation(jax.random.fold_in(keys[4], 3), CONTACTS // CONT_DEV)
    contact_tile = jax.vmap(lambda own, number: shared_out(jax.random.fold_in(keys[4], 2), own, number, CONT_DEV, N_LEN, 1, CAP, 2))(contact_tile_keys, contact_tile_turns).reshape((CONTACTS, 1))
    contact_row = with_ends(jax.random.randint(keys[5], (CONTACTS,), 0, CX * NY), jax.random.fold_in(keys[5], 1), 0, (CX * NY) - 1).astype(jnp.int32)
    contact_force = noise(keys[6], (CONTACTS, 3, NZ), 1.0, 6.0, ((0, 64),), jnp.float32)
    return {"predicted": predicted, "material": material, "stiffness_table": stiffness_table, "density_table": density_table, "contact_tile": contact_tile, "contact_row": contact_row, "contact_force": contact_force}


AXIAL_RATIO = 12.0
SWEEP_GAIN = 56.0
MASS_SHIFT = 0.05
RELAXATION = 0.7

def stencil_core(padded, level_scale):
    centre = padded[:, 1:-1, 1:-1, 1:-1]
    along_x = padded[:, 2:, 1:-1, 1:-1] + padded[:, :-2, 1:-1, 1:-1]
    across = padded[:, 1:-1, 2:, 1:-1] + padded[:, 1:-1, :-2, 1:-1]
    depth_sum = padded[:, 1:-1, 1:-1, 2:] + padded[:, 1:-1, 1:-1, :-2]
    return (2.0 * AXIAL_RATIO + 2.0 + 2.0 * level_scale) * centre - AXIAL_RATIO * along_x - across - level_scale * depth_sum

def pad_all(source):
    return jnp.pad(source, ((0, 0), (1, 1), (1, 1), (1, 1)))

def diagonal(stiff_root, inertia, level_scale):
    return level_scale * inertia + stiff_root * stiff_root * (2.0 * AXIAL_RATIO + 2.0 + 2.0 * level_scale)

def operate(motion, stiff_root, inertia, level_scale):
    lap_term = stencil_core(pad_all(stiff_root * motion), level_scale)
    return level_scale * inertia * motion + stiff_root * lap_term

def jacobi(motion, forcing, stiff_root, inertia, level_scale):
    image = operate(motion, stiff_root, inertia, level_scale)
    return motion + RELAXATION * (forcing - image) / diagonal(stiff_root, inertia, level_scale)

def restrict(source):
    return source.reshape(source.shape[0], source.shape[1] // 2, 2, source.shape[2] // 2, 2, source.shape[3]).sum(axis=(2, 4))

def coarsen(source):
    return source.reshape(source.shape[0] // 2, 2, source.shape[1] // 2, 2, source.shape[2]).mean(axis=(1, 3))

def prolong(source):
    return jnp.repeat(jnp.repeat(source, 2, axis=1), 2, axis=2)

def line_sweep(old_values, defect, stiff_root, inertia, level_scale):
    diag_term = diagonal(stiff_root, inertia, level_scale)
    padded = pad_all(stiff_root * old_values)
    right_side = padded[:, 2:, 1:-1, 1:-1]
    across = padded[:, 1:-1, 2:, 1:-1] + padded[:, 1:-1, :-2, 1:-1]
    depth_sum = padded[:, 1:-1, 1:-1, 2:] + padded[:, 1:-1, 1:-1, :-2]
    offset_term = (defect + stiff_root * (AXIAL_RATIO * right_side + across + level_scale * depth_sum)) / diag_term
    gain_term = SWEEP_GAIN * stiff_root / diag_term

    def advance(carried, items):
        offset_here, gain_here, root_here = items
        value_here = offset_here + gain_here * carried
        return (root_here * value_here, value_here)
    start_carry = jnp.zeros((defect.shape[0], defect.shape[2], defect.shape[3]), jnp.float32)
    _, stacked = lax.scan(advance, start_carry, (jnp.moveaxis(offset_term, 1, 0), gain_term, stiff_root))
    return jnp.moveaxis(stacked, 0, 1)

def reference(predicted, material, stiffness_table, density_table, contact_tile, contact_row, contact_force):
    stiff_root = jnp.sqrt(stiffness_table)[material]
    inertia = density_table[material] * MASS_SHIFT
    tile_ids = contact_tile[:, 0]
    along_global = (tile_ids * CX + contact_row // NY).astype(jnp.int32)
    across_global = (contact_row % NY).astype(jnp.int32)
    wheel_load = jnp.zeros((3, NX, NY, NZ), jnp.float32)
    wheel_load = wheel_load.at[:, along_global, across_global, :].add(jnp.transpose(contact_force, (1, 0, 2)))
    forcing = inertia * predicted + wheel_load
    motion = jacobi(predicted, forcing, stiff_root, inertia, 1.0)
    motion = jacobi(motion, forcing, stiff_root, inertia, 1.0)
    defect = forcing - operate(motion, stiff_root, inertia, 1.0)
    defect_one = restrict(defect)
    root_one = coarsen(stiff_root)
    mass_one = coarsen(inertia)
    correction_one = RELAXATION * defect_one / diagonal(root_one, mass_one, 4.0)
    correction_one = jacobi(correction_one, defect_one, root_one, mass_one, 4.0)
    defect_two = restrict(defect_one - operate(correction_one, root_one, mass_one, 4.0))
    root_two = coarsen(root_one)
    mass_two = coarsen(mass_one)
    correction_two = line_sweep(jnp.zeros_like(defect_two), defect_two, root_two, mass_two, 16.0)
    correction_two = line_sweep(correction_two, defect_two, root_two, mass_two, 16.0)
    correction_one = correction_one + prolong(correction_two)
    correction_one = jacobi(correction_one, defect_one, root_one, mass_one, 4.0)
    correction_one = jacobi(correction_one, defect_one, root_one, mass_one, 4.0)
    motion = motion + prolong(correction_one)
    motion = jacobi(motion, forcing, stiff_root, inertia, 1.0)
    motion = jacobi(motion, forcing, stiff_root, inertia, 1.0)
    residual = forcing - operate(motion, stiff_root, inertia, 1.0)
    return (motion, residual)
```

```python
import jax
import jax.numpy as jnp
from jax import lax
from jax.experimental import pallas as pl
from jax.experimental.pallas import tpu as pltpu
from jax.sharding import PartitionSpec as P

MESH = pl.DeviceIdType.MESH
F32 = jnp.float32
BF16 = jnp.bfloat16
LEN, SEC = 64, 4
AROUND = [(0, 1), (0, -1), (1, 0), (-1, 0), (1, 1), (1, -1), (-1, 1), (-1, -1)]
XE, TF = 32, 6
X1, T1 = 16, 3
X2 = 8


def shift_depth(w):
    lane = lax.broadcasted_iota(jnp.int32, w.shape, w.ndim - 1)
    low = jnp.where(lane == 0, 0.0, pltpu.roll(w, 1, w.ndim - 1))
    high = jnp.where(lane == 127, 0.0, pltpu.roll(w, 127, w.ndim - 1))
    return low + high


def shift_rows(w):
    tiles = w.shape[0]
    below = jnp.concatenate([pltpu.roll(w[tiles - 1 :], 1, 1), w[: tiles - 1]], axis=0)
    above = jnp.concatenate([w[1:], pltpu.roll(w[:1], 7, 1)], axis=0)
    return below + above


def around(ref, c, x, scale):
    w = ref[c, x]
    along = ref[c, x - 1] + ref[c, x + 1]
    depth = shift_depth(w)
    if scale != 1.0:
        depth = scale * depth
    return w, 12.0 * along + (shift_rows(w) + depth)


def halves(value):
    high = value.astype(BF16)
    return high, (value - high.astype(F32)).astype(BF16)


def body(
    pred, mat, stiff, dens, tile, crow, force,
    out_v, out_r,
    pext, mext, sent, got, got_l, got_r,
    q0, m0, b0, ra0, e0, iq0,
    wa, wb, ff, aa,
    q1, m1, b1, ra1, e1, iq1,
    d1, a1, wc, wd, nat, deft,
    fac2, rq2, q2, iq2,
    slope_y, slope_z, g1, g2, z1, z2,
    s_first, r_first, s_ends, r_right, r_left,
    w1s, up_s, dn_s, up_r, dn_r,
    v2s, va_s, vb_s, va_r, vb_r, pn, on_v, on_r,
    sem_in, e_s, e_r, a_s, a_r, f_s, f_r, gs, gr, zs, zr, n_s, n_r, x_s, x_r, o_s,
):
    l = lax.axis_index("len")
    s = lax.axis_index("sec")
    z = l // 8
    r = lax.rem(l, 8)

    def there(dl, ds):
        return {
            "len": jnp.clip(l + dl, 0, LEN - 1),
            "sec": jnp.clip(s + ds, 0, SEC - 1),
        }

    def has(dl, ds):
        a, b = l + dl, s + ds
        return (a >= 0) & (a < LEN) & (b >= 0) & (b < SEC)

    def remote(src, dst, ssem, rsem, device):
        return pltpu.make_async_remote_copy(
            src_ref=src, dst_ref=dst, send_sem=ssem, recv_sem=rsem,
            device_id=device, device_id_type=MESH,
        )

    class Send:
        def __init__(self, src, dst, ssem, rsem, dl, ds):
            self.copy = remote(src, dst, ssem, rsem, there(dl, ds))
            self.to, self.back = has(dl, ds), has(-dl, -ds)

        def start(self):
            pl.when(self.to)(self.copy.start)

        def sent(self):
            pl.when(self.to)(self.copy.wait_send)

        def came(self):
            pl.when(self.back)(self.copy.wait_recv)

    late = []

    own_p = pltpu.make_async_copy(pred, pext.at[:, 8:24, 8:40, :], sem_in.at[0])
    own_m = pltpu.make_async_copy(mat, mext.at[8:24, 8:40, :], sem_in.at[1])
    own_p.start()
    own_m.start()

    def clear(ref, *at):
        shape = ref.at[at].shape if at else ref.shape
        ref[at if at else ...] = jnp.zeros(shape, ref.dtype)

    edge_l, edge_r, edge_d, edge_u = l == 0, l == LEN - 1, s == 0, s == SEC - 1
    every = slice(None)

    def clear_x(lo, hi):
        def step(x, _):
            for c in range(3):
                pext[c, x] = jnp.zeros((48, 128), F32)
            mext[x] = jnp.zeros((48, 128), jnp.int32)
            return 0

        lax.fori_loop(lo, hi, step, 0)

    def clear_rows(lo):
        def step(x, _):
            for c in range(3):
                pext[c, x, lo : lo + 8, :] = jnp.zeros((8, 128), F32)
            mext[x, lo : lo + 8, :] = jnp.zeros((8, 128), jnp.int32)
            return 0

        lax.fori_loop(0, XE, step, 0)

    @pl.when(edge_l)
    def _():
        clear_x(0, 8)
        clear(got_l)
        clear(r_left)

    @pl.when(edge_r)
    def _():
        clear_x(24, 32)
        clear(got_r)
        clear(r_first)
        clear(r_right)

    @pl.when(edge_d)
    def _():
        clear_rows(0)
        clear(up_r)
        clear(va_r)

    @pl.when(edge_u)
    def _():
        clear_rows(40)
        clear(dn_r)
        clear(vb_r)

    @pl.when(edge_l | edge_r | edge_d | edge_u)
    def _():
        def step(i, _):
            for k in range(2):
                for c in range(3):
                    nat[k, c, i] = jnp.zeros((24, 128), F32)
            return 0

        lax.fori_loop(0, X1, step, 0)

    barrier = pltpu.get_barrier_semaphore()

    def greet(k, _):
        pl.semaphore_signal(
            barrier, inc=1, device_id_type=MESH,
            device_id={"len": lax.rem(l + k, LEN), "sec": s},
        )
        return 0

    lax.fori_loop(1, LEN, greet, 0)
    met = LEN - 1
    for dl, ds in AROUND:
        if ds:
            met = met + jnp.where(has(dl, ds), 1, 0)

            @pl.when(has(dl, ds))
            def _(dl=dl, ds=ds):
                pl.semaphore_signal(barrier, inc=1, device_id_type=MESH, device_id=there(dl, ds))

    column = lax.broadcasted_iota(jnp.int32, (64, 64), 0)
    matches = (tile[...] == column).astype(F32)
    earlier = (column < lax.broadcasted_iota(jnp.int32, (64, 64), 1)).astype(BF16)
    before = jnp.dot(matches.astype(BF16), earlier, preferred_element_type=F32)
    picks = [matches * (before == k).astype(F32) for k in (0.0, 1.0)]
    keys = (crow[...] + 1).astype(F32)
    select = jnp.concatenate(picks, axis=0).astype(BF16)
    flat = jnp.concatenate([force[c] for c in range(3)], axis=1)
    packed = jnp.dot(
        jnp.concatenate([select, select], axis=1),
        jnp.concatenate(halves(flat), axis=0),
        preferred_element_type=F32,
    )
    for k in range(2):
        for c in range(3):
            sent[pl.ds(4 * k + c, 64, stride=8), :] = packed[64 * k : 64 * k + 64, 128 * c : 128 * c + 128]
        here = jnp.sum(picks[k] * keys, axis=1, keepdims=True)
        sent[pl.ds(4 * k + 3, 64, stride=8), :] = jnp.broadcast_to(here, (64, 128))

    def rows_of(t):
        return pl.ds(pl.multiple_of(t * 8, 8), 8)

    pl.semaphore_wait(barrier, met)

    def post(k, _):
        t = lax.rem(l + k, LEN)
        remote(sent.at[rows_of(t)], got.at[rows_of(l)], a_s.at[0], a_r.at[0], {"len": t, "sec": s}).start()
        return 0

    lax.fori_loop(1, LEN, post, 0)
    got[rows_of(l), :] = sent[rows_of(l), :]

    halo = []
    for i, (dl, ds) in enumerate(AROUND):
        sx = {1: slice(8, 16), -1: slice(0, 8), 0: slice(0, 16)}[dl]
        dx = {1: slice(0, 8), -1: slice(24, 32), 0: slice(8, 24)}[dl]
        sy = {1: slice(24, 32), -1: slice(0, 8), 0: slice(0, 32)}[ds]
        dy = {1: slice(0, 8), -1: slice(40, 48), 0: slice(8, 40)}[ds]
        halo.append(Send(mat.at[sx, sy, :], mext.at[dx, dy, :], e_s.at[2 * i], e_r.at[2 * i], dl, ds))
        halo.append(Send(pred.at[:, sx, sy, :], pext.at[:, dx, dy, :], e_s.at[2 * i + 1], e_r.at[2 * i + 1], dl, ds))
    for h in halo[::2] + halo[1::2]:
        h.start()
    late += halo
    own_m.wait()
    for h in halo[::2]:
        h.came()

    sub = lax.broadcasted_iota(jnp.int32, (8, 128), 0)

    def inside(x, y):
        return (x >= 0) & (x < 16 * LEN) & (y >= 0) & (y < 32 * SEC)

    def fine_coefficients(x, _):
        for j in range(TF):
            ids = mext[x, pl.ds(j, 8, stride=TF), :]
            stiffness = jnp.full((8, 128), stiff[0], F32)
            density = jnp.full((8, 128), dens[0], F32)
            for entry in range(1, 8):
                stiffness = jnp.where(ids == entry, stiff[entry], stiffness)
                density = jnp.where(ids == entry, dens[entry], density)
            grid = inside(l * 16 + x - 8, s * 32 - 8 + sub * TF + j)
            q = jnp.sqrt(stiffness)
            m = 0.05 * density
            d = m + 28.0 * stiffness
            iq = 1.0 / q
            rd = jnp.where(grid, 0.7 / d, 0.0)
            q0[x, j] = q
            m0[x, j] = m
            b0[x, j] = rd * stiffness
            ra0[x, j] = rd * q
            e0[x, j] = d * iq
            iq0[x, j] = iq
        return 0

    lax.fori_loop(0, XE, fine_coefficients, 0)

    def one_coefficients(x, _):
        for j in range(T1):
            q = 0.25 * ((q0[2 * x, 2 * j] + q0[2 * x + 1, 2 * j]) + (q0[2 * x, 2 * j + 1] + q0[2 * x + 1, 2 * j + 1]))
            m = 0.25 * ((m0[2 * x, 2 * j] + m0[2 * x + 1, 2 * j]) + (m0[2 * x, 2 * j + 1] + m0[2 * x + 1, 2 * j + 1]))
            grid = inside(l * 16 + 2 * x - 8, s * 32 - 8 + (sub * T1 + j) * 2)
            d = 4.0 * m + 34.0 * (q * q)
            iq = 1.0 / q
            rd = jnp.where(grid, 0.7 / d, 0.0)
            q1[x, j] = q
            m1[x, j] = m
            b1[x, j] = rd * (q * q)
            ra1[x, j] = rd * q
            e1[x, j] = d * iq
            iq1[x, j] = iq
        return 0

    lax.fori_loop(0, X1, one_coefficients, 0)

    def own_rows_of_pairs(slot, tiles):
        for j in range(T1):
            pn[slot, pl.ds(j, 8, stride=T1), :] = tiles[j]
        return pn[slot, pl.ds(4, 8, stride=2), :] + pn[slot, pl.ds(5, 8, stride=2), :]

    def two_coefficients(x, _):
        q = 0.25 * own_rows_of_pairs(0, [q1[2 * x, j] + q1[2 * x + 1, j] for j in range(T1)])
        m = 0.25 * own_rows_of_pairs(1, [m1[2 * x, j] + m1[2 * x + 1, j] for j in range(T1)])
        at = l * 4 + x - 2
        rd = jnp.where((at >= 0) & (at < 4 * LEN), 1.0, 0.0) / (16.0 * m + 58.0 * (q * q))
        q2[x] = q
        iq2[x] = 1.0 / q
        rq2[x] = rd * q
        fac2[x] = 56.0 * (rd * (q * q))
        return 0

    lax.fori_loop(0, X2, two_coefficients, 0)

    def gather_y(ref, value, i):
        ref[r] = value
        copies = []
        for k in range(1, 8):
            to = z * 8 + lax.rem(r + k, 8)
            copies.append(remote(ref.at[r], ref.at[r], gs.at[i, k], gr.at[i, k], {"len": to, "sec": s}))
        for copy in copies:
            copy.start()

        def came():
            for copy in copies:
                copy.wait_recv()

        def gone():
            for copy in copies:
                copy.wait_send()

        return came, gone

    def gather_z(ref, value, i):
        ref[z] = value
        copies = []
        for k in range(1, 8):
            to = lax.rem(z + k, 8) * 8 + r
            copies.append(remote(ref.at[z], ref.at[z], zs.at[i, k], zr.at[i, k], {"len": to, "sec": s}))
        for k, copy in enumerate(copies, 1):
            pl.when(z + k < 8)(copy.start)

        def came():
            for k, copy in enumerate(copies, 1):
                pl.when(z >= k)(copy.wait_recv)

        def gone():
            for k, copy in enumerate(copies, 1):
                pl.when(z + k < 8)(copy.wait_send)

        return came, gone

    came, gone_y0 = gather_y(slope_y, (fac2[2] * fac2[3]) * (fac2[4] * fac2[5]), 0)

    own_p.wait()
    for h in halo[1::2]:
        h.came()

    def start_fine(x, _):
        for j in range(TF):
            grid = inside(l * 16 + x - 8, s * 32 - 8 + sub * TF + j)
            for c in range(3):
                value = jnp.where(grid, pext[c, x, pl.ds(j, 8, stride=TF), :], 0.0)
                wa[c, x, j] = q0[x, j] * value
                ff[c, x, j] = m0[x, j] * value
        return 0

    lax.fori_loop(0, XE, start_fine, 0)

    came()
    ahead = lax.fori_loop(0, r, lambda k, p: p * slope_y[k], jnp.ones((8, 128), F32))
    whole = lax.fori_loop(r, 8, lambda k, p: p * slope_y[k], ahead)
    came, gone_z0 = gather_z(slope_z, whole, 0)

    every_row = remote(sent.at[0:504], got.at[0:504], a_s.at[0], a_r.at[0], there(0, 0))
    every_row.wait_recv()
    onward = [
        Send(got, got_l, f_s.at[0], f_r.at[0], 1, 0),
        Send(got, got_r, f_s.at[1], f_r.at[1], -1, 0),
    ]
    for h in onward:
        h.start()
    late += onward

    def add_loads(ref, block, first, x_local):
        lane = lax.broadcasted_iota(jnp.int32, (64, 128), 1)
        source = lax.broadcasted_iota(jnp.int32, (64, 128), 0)
        key = jnp.zeros((1, 128), F32)
        for k in range(2):
            rows = ref[pl.ds(4 * k + 3, 64, stride=8), :]
            key = key + jnp.sum(jnp.where(lane == source + 64 * k, rows, 0.0), axis=0, keepdims=True)
        flat = jnp.concatenate(
            [
                jnp.concatenate([ref[pl.ds(4 * k + c, 64, stride=8), :] for k in range(2)], axis=0)
                for c in range(3)
            ],
            axis=1,
        )
        values = jnp.concatenate(halves(flat), axis=0)
        shape = (4, TF, 8, 128)
        row = s * 32 - 8 + lax.broadcasted_iota(jnp.int32, shape, 2) * TF + lax.broadcasted_iota(jnp.int32, shape, 1)
        for part in range(2):
            cell = lax.broadcasted_iota(jnp.int32, shape, 0) + (x_local + 4 * part)
            cell = jnp.where((row >= 0) & (row < 32 * SEC), cell * 128 + row + 1, -1)
            hit = (cell.astype(F32) == key.reshape(1, 1, 1, 128)).astype(F32)
            hit = hit.reshape(4 * TF * 8, 128).astype(BF16)
            loads = jnp.dot(jnp.concatenate([hit, hit], axis=1), values, preferred_element_type=F32)
            at = first + 4 * part
            for c in range(3):
                total = ff[c, pl.ds(at, 4)] + loads[:, 128 * c : 128 * c + 128].reshape(shape)
                ff[c, pl.ds(at, 4)] = total
                aa[c, pl.ds(at, 4)] = ra0[pl.ds(at, 4)] * total

    add_loads(got, 0, 8, 0)
    add_loads(got, 1, 16, 8)
    onward[0].came()
    add_loads(got_l, 2, 0, 8)
    onward[1].came()
    add_loads(got_r, 3, 24, 0)

    def fine_sweep(src, dst, lo, hi):
        def step(x, _):
            for c in range(3):
                w, n = around(src, c, x, 1.0)
                dst[c, x] = (0.3 * w + aa[c, x]) + b0[x] * n
            return 0

        lax.fori_loop(lo, hi, step, 0)

    fine_sweep(wa, wb, 1, 31)
    fine_sweep(wb, wa, 2, 30)

    def defect_one(x, _):
        for c in range(3):
            total = None
            for i in range(2):
                at = 2 * x + i
                w, n = around(wa, c, at, 1.0)
                d = (ff[c, at] - e0[at] * w) + q0[at] * n
                total = d if total is None else total + d
            for j in range(T1):
                here = total[2 * j] + total[2 * j + 1]
                d1[c, x, j] = here
                a1[c, x, j] = ra1[x, j] * here
        return 0

    lax.fori_loop(2, 14, defect_one, 0)

    def first_correction(x, _):
        for c in range(3):
            w, n = around(a1, c, x, 4.0)
            wc[c, x] = 1.3 * w + b1[x] * n
        return 0

    lax.fori_loop(3, 13, first_correction, 0)

    def keep_own(x, _):
        for c in range(3):
            for k, ref in enumerate((a1, wc)):
                for j in range(T1):
                    pn[2 * c + k, pl.ds(j, 8, stride=T1), :] = ref[c, x, j]
                nat[k, c, x, 4:20, :] = pn[2 * c + k, 4:20, :]
        return 0

    for c in range(3):
        for x2 in range(4):
            total = None
            for i in range(2):
                x = 4 + 2 * x2 + i
                w, n = around(wc, c, x, 4.0)
                d = (d1[c, x] - e1[x] * w) + q1[x] * n
                total = d if total is None else total + d
            deft[c, x2] = own_rows_of_pairs(4 * c + x2, [total[j] for j in range(T1)])

    came()
    whole_z = jnp.ones((8, 128), F32)
    f = [fac2[x] for x in range(X2)]

    def chain(off):
        total = off[0]
        for x in range(1, 4):
            total = off[x] + f[2 + x] * total
        return total

    def carried_in(ref_y, came_y, ref_z, i):
        came_y()

        def join(k, total):
            return tuple(ref_y[k, c] + slope_y[k] * total[c] for c in range(3))

        zero = tuple(jnp.zeros((8, 128), F32) for _ in range(3))
        mine = lax.fori_loop(0, r, join, zero)
        whole = lax.fori_loop(r, 8, join, mine)
        came_z, gone_z = gather_z(ref_z, jnp.stack(whole), i)

        def finish():
            came_z()

            def join_z(k, total):
                return tuple(ref_z[k, c] + slope_z[k] * total[c] for c in range(3))

            before = lax.fori_loop(0, z, join_z, zero)
            return [mine[c] + ahead * before[c] for c in range(3)]

        return finish, gone_z

    off = [[rq2[2 + x] * deft[c, x] for x in range(4)] for c in range(3)]
    came, gone_y1 = gather_y(g1, jnp.stack([chain(off[c]) for c in range(3)]), 1)
    for c in range(3):
        s_first[c] = off[c][0]
    first = Send(s_first, r_first, n_s.at[0], n_r.at[0], -1, 0)
    first.start()
    late.append(first)

    lax.fori_loop(4, 12, keep_own, 0)
    nat_up = Send(nat.at[:, :, 4:12, 16:20, :], nat.at[:, :, 4:12, 0:4, :], x_s.at[0], x_r.at[0], 0, 1)
    nat_dn = Send(nat.at[:, :, 4:12, 4:8, :], nat.at[:, :, 4:12, 20:24, :], x_s.at[1], x_r.at[1], 0, -1)
    nat_up.start()
    nat_dn.start()
    late += [nat_up, nat_dn]

    finish, gone_z1 = carried_in(g1, came, z1, 1)
    nat_up.came()
    nat_dn.came()
    nat_right = Send(nat.at[:, :, 8:12], nat.at[:, :, 0:4], x_s.at[2], x_r.at[2], 1, 0)
    nat_left = Send(nat.at[:, :, 4:8], nat.at[:, :, 12:16], x_s.at[3], x_r.at[3], -1, 0)
    nat_right.start()
    nat_left.start()
    late += [nat_right, nat_left]
    first.came()
    carry = finish()

    w1 = []
    for c in range(3):
        line = []
        at = carry[c]
        for x in range(4):
            at = off[c][x] + f[2 + x] * at
            line.append(at)
        line.append(r_first[c] + f[6] * at)
        w1.append(line)
    for i in range(12):
        w1s[8 * i : 8 * i + 8, :] = w1[i // 4][i % 4]
    w1s[96:128, :] = jnp.zeros((32, 128), F32)
    up_s[...] = w1s[pl.ds(7, 16, stride=8), :]
    dn_s[...] = w1s[pl.ds(0, 16, stride=8), :]
    rows_up = Send(up_s, up_r, n_s.at[1], n_r.at[1], 0, 1)
    rows_dn = Send(dn_s, dn_r, n_s.at[2], n_r.at[2], 0, -1)
    rows_up.start()
    rows_dn.start()
    late += [rows_up, rows_dn]
    depth = [[16.0 * shift_depth(w1[c][x]) for x in range(4)] for c in range(3)]
    rows_up.came()
    rows_dn.came()
    off = []
    for c in range(3):
        line = []
        for x in range(4):
            i = 4 * c + x
            w = w1[c][x]
            below = jnp.where(sub == 0, up_r[i : i + 1, :], pltpu.roll(w, 1, 0))
            above = jnp.where(sub == 7, dn_r[i : i + 1, :], pltpu.roll(w, 7, 0))
            n = 12.0 * w1[c][x + 1] + ((below + above) + depth[c][x])
            line.append(rq2[2 + x] * (deft[c, x] + q2[2 + x] * n))
        off.append(line)

    came, gone_y2 = gather_y(g2, jnp.stack([chain(off[c]) for c in range(3)]), 2)
    for c in range(3):
        s_ends[c, 0] = off[c][0]
        s_ends[c, 1] = off[c][1]
        s_ends[c, 2] = off[c][3]
    to_left = Send(s_ends.at[:, 0:2], r_right, n_s.at[3], n_r.at[3], -1, 0)
    to_right = Send(s_ends.at[:, 2:3], r_left, n_s.at[4], n_r.at[4], 1, 0)
    to_left.start()
    to_right.start()
    late += [to_left, to_right]
    finish, gone_z2 = carried_in(g2, came, z2, 2)
    to_left.came()
    to_right.came()
    nat_right.came()
    nat_left.came()
    carry = finish()

    back = jnp.where(l > 0, 1.0, 0.0) / jnp.where(l > 0, f[1], 1.0)
    for c in range(3):
        line = [(carry[c] - r_left[c, 0]) * back, carry[c]]
        at = carry[c]
        for x in range(6):
            shift = off[c][x] if x < 4 else r_right[c, x - 4]
            at = shift + f[2 + x] * at
            line.append(at)
        for x in range(X2):
            i = 8 * (c * X2 + x)
            v2s[i : i + 8, :] = iq2[x] * line[x]
    for k in range(2):
        va_s[24 * k : 24 * k + 24, :] = v2s[pl.ds(6 + k, 24, stride=8), :]
        vb_s[24 * k : 24 * k + 24, :] = v2s[pl.ds(k, 24, stride=8), :]
    ends_up = Send(va_s, va_r, n_s.at[5], n_r.at[5], 0, 1)
    ends_dn = Send(vb_s, vb_r, n_s.at[6], n_r.at[6], 0, -1)
    ends_up.start()
    ends_dn.start()
    late += [ends_up, ends_dn]

    for i in range(24):
        v = v2s[8 * i : 8 * i + 8, :]
        pn[i, pl.ds(4, 8, stride=2), :] = v
        pn[i, pl.ds(5, 8, stride=2), :] = v
    ends_up.came()
    ends_dn.came()
    for i in range(24):
        for k in range(2):
            pn[i, 2 * k : 2 * k + 2, :] = jnp.broadcast_to(va_r[24 * k + i : 24 * k + i + 1, :], (2, 128))
            pn[i, 20 + 2 * k : 22 + 2 * k, :] = jnp.broadcast_to(vb_r[24 * k + i : 24 * k + i + 1, :], (2, 128))

    def correct_one(x2, _):
        for c in range(3):
            for j in range(T1):
                v = pn[c * X2 + x2, pl.ds(j, 8, stride=T1), :]
                for i in range(2):
                    x = 2 * x2 + i
                    a1[c, x, j] = nat[0, c, x, pl.ds(j, 8, stride=T1), :]
                    wc[c, x, j] = nat[1, c, x, pl.ds(j, 8, stride=T1), :] + q1[x, j] * v
        return 0

    lax.fori_loop(0, X2, correct_one, 0)

    def one_sweep(src, dst, lo, hi):
        def step(x, _):
            for c in range(3):
                w, n = around(src, c, x, 4.0)
                dst[c, x] = (0.3 * w + a1[c, x]) + b1[x] * n
            return 0

        lax.fori_loop(lo, hi, step, 0)

    one_sweep(wc, wd, 1, 15)
    one_sweep(wd, wc, 2, 14)

    def correct_fine(x, _):
        for c in range(3):
            v = iq1[x] * wc[c, x]
            for i in range(2):
                for j in range(TF):
                    at = 2 * x + i
                    wb[c, at, j] = wa[c, at, j] + q0[at, j] * v[j // 2]
        return 0

    lax.fori_loop(2, 14, correct_fine, 0)
    fine_sweep(wb, wa, 5, 27)
    fine_sweep(wa, wb, 6, 26)

    def results(x, _):
        for c in range(3):
            w, n = around(wb, c, x, 1.0)
            value = iq0[x] * w
            rest = (ff[c, x] - e0[x] * w) + q0[x] * n
            for j in range(TF):
                on_v[c, x - 8, pl.ds(j, 8, stride=TF), :] = value[j]
                on_r[c, x - 8, pl.ds(j, 8, stride=TF), :] = rest[j]
        return 0

    lax.fori_loop(8, 24, results, 0)
    outs = [
        pltpu.make_async_copy(on_v.at[:, :, 8:40, :], out_v, o_s.at[0]),
        pltpu.make_async_copy(on_r.at[:, :, 8:40, :], out_r, o_s.at[1]),
    ]
    for copy in outs:
        copy.start()
    every_row.wait_send()
    for h in late:
        h.sent()
    for gone in (gone_y0, gone_z0, gone_y1, gone_z1, gone_y2, gone_z2):
        gone()
    for copy in outs:
        copy.wait()


def shards(predicted, material, stiffness, density, tile, row, force):
    anywhere = pl.BlockSpec(memory_space=pl.ANY)
    vmem = pl.BlockSpec(memory_space=pltpu.VMEM)
    smem = pl.BlockSpec(memory_space=pltpu.SMEM)

    def v(*shape, dtype=F32):
        return pltpu.VMEM(shape, dtype)

    dma = pltpu.SemaphoreType.DMA
    scratch = [
        v(3, XE, 48, 128), v(XE, 48, 128, dtype=jnp.int32),
        v(512, 128), v(512, 128), v(512, 128), v(512, 128),
        *[v(XE, TF, 8, 128) for _ in range(6)],
        *[v(3, XE, TF, 8, 128) for _ in range(4)],
        *[v(X1, T1, 8, 128) for _ in range(6)],
        *[v(3, X1, T1, 8, 128) for _ in range(4)],
        v(2, 3, X1, 24, 128), v(3, 4, 8, 128),
        *[v(X2, 8, 128) for _ in range(4)],
        v(8, 8, 128), v(8, 8, 128),
        *[v(8, 3, 8, 128) for _ in range(4)],
        v(3, 8, 128), v(3, 8, 128), v(3, 3, 8, 128), v(3, 2, 8, 128), v(3, 1, 8, 128),
        v(128, 128), *[v(16, 128) for _ in range(4)],
        v(192, 128), *[v(48, 128) for _ in range(4)],
        v(24, 24, 128), v(3, 16, 48, 128), v(3, 16, 48, 128),
        dma((2,)), dma((16,)), dma((16,)), dma((1,)), dma((1,)), dma((2,)), dma((2,)),
        dma((3, 8)), dma((3, 8)), dma((3, 8)), dma((3, 8)),
        dma((7,)), dma((7,)), dma((4,)), dma((4,)), dma((2,)),
    ]
    result = jax.ShapeDtypeStruct(predicted.shape, F32)
    return pl.pallas_call(
        body,
        out_shape=(result, result),
        in_specs=[anywhere, anywhere, smem, smem, vmem, vmem, vmem],
        out_specs=(anywhere, anywhere),
        scratch_shapes=scratch,
        compiler_params=pltpu.CompilerParams(
            collective_id=0, has_side_effects=True, vmem_limit_bytes=48 * 2**20
        ),
    )(
        predicted, material, stiffness, density,
        tile.reshape(1, -1), row.reshape(1, -1), jnp.transpose(force, (1, 0, 2)),
    )


def solution(mesh):
    placed = (
        P(None, "len", "sec", None),
        P("len", "sec", None),
        P(),
        P(),
        P("len", None),
        P("len"),
        P("len", None, None),
    )
    return jax.shard_map(
        shards,
        mesh=mesh,
        in_specs=placed,
        out_specs=(P(None, "len", "sec", None), P(None, "len", "sec", None)),
        check_vma=False,
    )
```

```python
import jax
import jax.numpy as jnp
from jax import lax
from jax.experimental import pallas as pl
from jax.experimental.pallas import tpu as pltpu
from jax.sharding import PartitionSpec as P

MESH = pl.DeviceIdType.MESH
F32 = jnp.float32
BF16 = jnp.bfloat16
LEN, SEC = 64, 4
FINE_GROUP, ONE_GROUP = 4, 7
FAR_FIRST = [4, 3, 5, 2, 6, 1, 7, 0]
XE, TF = 32, 6
X1, T1 = 16, 3
X2 = 8


def shift_depth(w):
    lane = lax.broadcasted_iota(jnp.int32, w.shape, w.ndim - 1)
    low = jnp.where(lane == 0, 0.0, pltpu.roll(w, 1, w.ndim - 1))
    high = jnp.where(lane == 127, 0.0, pltpu.roll(w, 127, w.ndim - 1))
    return low + high


def shift_rows(w):
    last = w.shape[1] - 1
    below = jnp.concatenate([pltpu.roll(w[:, last:], 1, 2), w[:, :last]], axis=1)
    above = jnp.concatenate([w[:, 1:], pltpu.roll(w[:, :1], 7, 2)], axis=1)
    return below + above


def around(ref, c, x, count, scale):
    block = ref[c, pl.ds(x - 1, count + 2)]
    w = block[1:-1]
    depth = shift_depth(w)
    if scale != 1.0:
        depth = scale * depth
    return w, 12.0 * (block[:-2] + block[2:]) + (shift_rows(w) + depth)


def over(lo, hi, group, step):
    rest = (hi - lo) % group
    if rest:
        step(lo, rest)
    if hi - lo - rest == group:
        step(lo + rest, group)
    elif hi - lo > rest:

        def turn(i, _):
            step(lo + rest + i * group, group)
            return 0

        lax.fori_loop(0, (hi - lo) // group, turn, 0)


def halves(value):
    high = value.astype(BF16)
    return high, (value - high.astype(F32)).astype(BF16)


def body(
    pred, mat, stiff, dens, tile, crow, force,
    out_v, out_r,
    pext, mext, sent, got, got_l, got_r,
    q0, m0, b0, ra0, e0, iq0,
    wa, wb, ff, aa,
    q1, m1, b1, ra1, e1, iq1,
    d1, a1, wc, wd, nat, deft,
    fac2, rq2, q2, iq2,
    slope_y, slope_z, g1, g2, z1, z2,
    s_first, r_first, s_ends, r_right, r_left,
    w1s, up_s, dn_s, up_r, dn_r,
    v2s, va_s, vb_s, va_r, vb_r, pn, on_v, on_r,
    sem_in, e_s, e_r, a_s, a_r, f_s, f_r, gs, gr, zs, zr, n_s, n_r, x_s, x_r, o_s,
):
    l = lax.axis_index("len")
    s = lax.axis_index("sec")
    z = l // 8
    r = lax.rem(l, 8)

    def there(dl, ds):
        return {
            "len": jnp.clip(l + dl, 0, LEN - 1),
            "sec": jnp.clip(s + ds, 0, SEC - 1),
        }

    def has(dl, ds):
        a, b = l + dl, s + ds
        return (a >= 0) & (a < LEN) & (b >= 0) & (b < SEC)

    def remote(src, dst, ssem, rsem, device):
        return pltpu.make_async_remote_copy(
            src_ref=src, dst_ref=dst, send_sem=ssem, recv_sem=rsem,
            device_id=device, device_id_type=MESH,
        )

    class Send:
        def __init__(self, src, dst, ssem, rsem, dl, ds):
            self.copy = remote(src, dst, ssem, rsem, there(dl, ds))
            self.to, self.back = has(dl, ds), has(-dl, -ds)

        def start(self):
            pl.when(self.to)(self.copy.start)

        def sent(self):
            pl.when(self.to)(self.copy.wait_send)

        def came(self):
            pl.when(self.back)(self.copy.wait_recv)

    late = []

    own_p = pltpu.make_async_copy(pred, pext.at[:, 8:24, 8:40, :], sem_in.at[0])
    own_m = pltpu.make_async_copy(mat, mext.at[8:24, 8:40, :], sem_in.at[1])
    own_p.start()
    own_m.start()

    def clear(ref):
        ref[...] = jnp.zeros(ref.shape, ref.dtype)

    barrier = pltpu.get_barrier_semaphore()

    def greet_at(where):
        pl.semaphore_signal(barrier, inc=1, device_id=where, device_id_type=MESH)

    def greet(k, _):
        greet_at({"len": lax.rem(l + k, LEN), "sec": s})
        return 0

    lax.fori_loop(2, LEN - 1, greet, 0)

    def clear_x(x, _):
        for c in range(3):
            for side in (0, 24):
                pext[c, side + x] = jnp.zeros((48, 128), F32)
        for side in (0, 24):
            mext[side + x] = jnp.zeros((48, 128), jnp.int32)
        return 0

    lax.fori_loop(0, 8, clear_x, 0)

    def clear_rows(x, _):
        for side in (0, 40):
            for c in range(3):
                pext[c, x, side : side + 8, :] = jnp.zeros((8, 128), F32)
            mext[x, side : side + 8, :] = jnp.zeros((8, 128), jnp.int32)
        return 0

    lax.fori_loop(8, 24, clear_rows, 0)

    @pl.when(l == 0)
    def _():
        clear(got_l)
        clear(r_left)

    @pl.when(l == LEN - 1)
    def _():
        clear(got_r)
        clear(r_first)
        clear(r_right)

    @pl.when(s == 0)
    def _():
        clear(up_r)
        clear(va_r)

    @pl.when(s == SEC - 1)
    def _():
        clear(dn_r)
        clear(vb_r)

    @pl.when((l == 0) | (l == LEN - 1) | (s == 0) | (s == SEC - 1))
    def _():
        def step(i, _):
            for k in range(2):
                for c in range(3):
                    nat[k, c, i] = jnp.zeros((24, 128), F32)
            return 0

        lax.fori_loop(0, X1, step, 0)

    for k in (1, LEN - 1):
        greet(k, 0)
    met = LEN - 1
    for ds in (1, -1):
        met = met + jnp.where(has(0, ds), 1, 0)
        pl.when(has(0, ds))(lambda ds=ds: greet_at(there(0, ds)))

    column = lax.broadcasted_iota(jnp.int32, (64, 64), 0)
    matches = (tile[...] == column).astype(F32)
    earlier = (column < lax.broadcasted_iota(jnp.int32, (64, 64), 1)).astype(BF16)
    before = jnp.dot(matches.astype(BF16), earlier, preferred_element_type=F32)
    picks = [matches * (before == k).astype(F32) for k in (0.0, 1.0)]
    keys = (crow[...] + 1).astype(F32)
    select = jnp.concatenate(picks, axis=0).astype(BF16)
    flat = jnp.concatenate([force[c] for c in range(3)], axis=1)
    packed = jnp.dot(
        jnp.concatenate([select, select], axis=1),
        jnp.concatenate(halves(flat), axis=0),
        preferred_element_type=F32,
    )
    for k in range(2):
        for c in range(3):
            sent[pl.ds(4 * k + c, 64, stride=8), :] = packed[64 * k : 64 * k + 64, 128 * c : 128 * c + 128]
        here = jnp.sum(picks[k] * keys, axis=1, keepdims=True)
        sent[pl.ds(4 * k + 3, 64, stride=8), :] = jnp.broadcast_to(here, (64, 128))

    def rows_of(t):
        return pl.ds(pl.multiple_of(t * 8, 8), 8)

    pl.semaphore_wait(barrier, met)

    def plane(g):
        return lax.rem(z + g, 8)

    for g in FAR_FIRST:

        def post(i, _, g=g):
            t = plane(g) * 8 + lax.rem(r + i, 8)
            remote(sent.at[rows_of(t)], got.at[rows_of(l)], a_s.at[0], a_r.at[g], {"len": t, "sec": s}).start()
            return 0

        lax.fori_loop(0 if g else 1, 8, post, 0)
    got[rows_of(l), :] = sent[rows_of(l), :]

    def halo(number, source, target, dl, ds):
        return Send(source, target, e_s.at[number], e_r.at[number], dl, ds)

    mat_sec = [
        halo(0, mat.at[:, 24:32, :], mext.at[8:24, 0:8, :], 0, 1),
        halo(1, mat.at[:, 0:8, :], mext.at[8:24, 40:48, :], 0, -1),
    ]
    pred_sec = [
        halo(2, pred.at[:, :, 25:32, :], pext.at[:, 8:24, 1:8, :], 0, 1),
        halo(3, pred.at[:, :, 0:7, :], pext.at[:, 8:24, 40:47, :], 0, -1),
    ]
    mat_len = [
        halo(4, mat.at[8:16], mext.at[0:8, 8:40, :], 1, 0),
        halo(5, mat.at[0:8], mext.at[24:32, 8:40, :], -1, 0),
    ]
    pred_len = [
        halo(6, pred.at[:, 9:16], pext.at[:, 1:8, 8:40, :], 1, 0),
        halo(7, pred.at[:, 0:7], pext.at[:, 24:31, 8:40, :], -1, 0),
    ]
    mat_corners, pred_corners = [], []
    for i, (mrows, prows) in enumerate([(slice(0, 8), slice(2, 8)), (slice(40, 48), slice(40, 46))]):
        mat_corners.append(halo(8 + i, mext.at[18:24, mrows, :], mext.at[2:8, mrows, :], 1, 0))
        mat_corners.append(halo(10 + i, mext.at[8:14, mrows, :], mext.at[24:30, mrows, :], -1, 0))
        pred_corners.append(halo(12 + i, pext.at[:, 18:24, prows, :], pext.at[:, 2:8, prows, :], 1, 0))
        pred_corners.append(halo(14 + i, pext.at[:, 8:14, prows, :], pext.at[:, 24:30, prows, :], -1, 0))

    def start(copies):
        for copy in copies:
            copy.start()
        late.extend(copies)

    def arrive(copies):
        for copy in copies:
            copy.came()

    start(mat_sec)
    start(pred_sec)
    start(mat_len)
    start(pred_len)
    own_m.wait()
    arrive(mat_sec)
    start(mat_corners)

    sub = lax.broadcasted_iota(jnp.int32, (8, 128), 0)

    def inside(x, y):
        return (x >= 0) & (x < 16 * LEN) & (y >= 0) & (y < 32 * SEC)

    def fine_coefficients(x, _):
        for j in range(TF):
            ids = mext[x, pl.ds(j, 8, stride=TF), :]
            stiffness = jnp.full((8, 128), stiff[0], F32)
            density = jnp.full((8, 128), dens[0], F32)
            for entry in range(1, 8):
                stiffness = jnp.where(ids == entry, stiff[entry], stiffness)
                density = jnp.where(ids == entry, dens[entry], density)
            grid = inside(l * 16 + x - 8, s * 32 - 8 + sub * TF + j)
            q = jnp.sqrt(stiffness)
            m = 0.05 * density
            d = m + 28.0 * stiffness
            iq = 1.0 / q
            rd = jnp.where(grid, 0.7 / d, 0.0)
            q0[x, j] = q
            m0[x, j] = m
            b0[x, j] = rd * stiffness
            ra0[x, j] = rd * q
            e0[x, j] = d * iq
            iq0[x, j] = iq
        return 0

    lax.fori_loop(8, 24, fine_coefficients, 0)

    def one_coefficients(x, _):
        for j in range(T1):
            q = 0.25 * ((q0[2 * x, 2 * j] + q0[2 * x + 1, 2 * j]) + (q0[2 * x, 2 * j + 1] + q0[2 * x + 1, 2 * j + 1]))
            m = 0.25 * ((m0[2 * x, 2 * j] + m0[2 * x + 1, 2 * j]) + (m0[2 * x, 2 * j + 1] + m0[2 * x + 1, 2 * j + 1]))
            grid = inside(l * 16 + 2 * x - 8, s * 32 - 8 + (sub * T1 + j) * 2)
            d = 4.0 * m + 34.0 * (q * q)
            iq = 1.0 / q
            rd = jnp.where(grid, 0.7 / d, 0.0)
            q1[x, j] = q
            m1[x, j] = m
            b1[x, j] = rd * (q * q)
            ra1[x, j] = rd * q
            e1[x, j] = d * iq
            iq1[x, j] = iq
        return 0

    lax.fori_loop(4, 12, one_coefficients, 0)

    def own_rows_of_pairs(slot, tiles):
        for j in range(T1):
            pn[slot, pl.ds(j, 8, stride=T1), :] = tiles[j]
        return pn[slot, pl.ds(4, 8, stride=2), :] + pn[slot, pl.ds(5, 8, stride=2), :]

    def two_coefficients(x, _):
        q = 0.25 * own_rows_of_pairs(0, [q1[2 * x, j] + q1[2 * x + 1, j] for j in range(T1)])
        m = 0.25 * own_rows_of_pairs(1, [m1[2 * x, j] + m1[2 * x + 1, j] for j in range(T1)])
        at = l * 4 + x - 2
        rd = jnp.where((at >= 0) & (at < 4 * LEN), 1.0, 0.0) / (16.0 * m + 58.0 * (q * q))
        q2[x] = q
        iq2[x] = 1.0 / q
        rq2[x] = rd * q
        fac2[x] = 56.0 * (rd * (q * q))
        return 0

    lax.fori_loop(2, 6, two_coefficients, 0)

    def gather_y(ref, value, i):
        ref[r] = value
        copies = []
        for k in range(1, 8):
            to = z * 8 + lax.rem(r + k, 8)
            copies.append(remote(ref.at[r], ref.at[r], gs.at[i, k], gr.at[i, k], {"len": to, "sec": s}))
        for copy in copies:
            copy.start()

        def came():
            for copy in copies:
                copy.wait_recv()

        def gone():
            for copy in copies:
                copy.wait_send()

        return came, gone

    def gather_z(ref, value, i):
        ref[z] = value
        copies = []
        for k in range(1, 8):
            to = lax.rem(z + k, 8) * 8 + r
            copies.append(remote(ref.at[z], ref.at[z], zs.at[i, k], zr.at[i, k], {"len": to, "sec": s}))
        for k, copy in enumerate(copies, 1):
            pl.when(z + k < 8)(copy.start)

        def came():
            for k, copy in enumerate(copies, 1):
                pl.when(z >= k)(copy.wait_recv)

        def gone():
            for k, copy in enumerate(copies, 1):
                pl.when(z + k < 8)(copy.wait_send)

        return came, gone

    came, gone_y0 = gather_y(slope_y, (fac2[2] * fac2[3]) * (fac2[4] * fac2[5]), 0)

    own_p.wait()
    arrive(pred_sec)
    start(pred_corners)

    def start_fine(x, _):
        for j in range(TF):
            grid = inside(l * 16 + x - 8, s * 32 - 8 + sub * TF + j)
            for c in range(3):
                value = jnp.where(grid, pext[c, x, pl.ds(j, 8, stride=TF), :], 0.0)
                wa[c, x, j] = q0[x, j] * value
                value = m0[x, j] * value
                ff[c, x, j] = value
                aa[c, x, j] = ra0[x, j] * value
        return 0

    lax.fori_loop(8, 24, start_fine, 0)

    def fine_sweep(src, dst, lo, hi):
        def step(x, count):
            at = pl.ds(x, count)
            for c in range(3):
                w, n = around(src, c, x, count, 1.0)
                dst[c, at] = (0.3 * w + aa[c, at]) + b0[at] * n

        over(lo, hi, FINE_GROUP, step)

    fine_sweep(wa, wb, 9, 23)

    came()
    ahead = lax.fori_loop(0, r, lambda k, p: p * slope_y[k], jnp.ones((8, 128), F32))
    whole = lax.fori_loop(r, 8, lambda k, p: p * slope_y[k], ahead)
    came, gone_z0 = gather_z(slope_z, whole, 0)

    for g in reversed(FAR_FIRST):
        few = remote(sent.at[0 : 64 if g else 56], got.at[0 : 64 if g else 56], a_s.at[0], a_r.at[g], there(0, 0))
        few.wait_recv()
        rows = pl.ds(pl.multiple_of(lax.rem(z + 8 - g, 8) * 64, 64), 64)
        Send(got.at[rows], got_l.at[rows], f_s.at[0], f_r.at[0], 1, 0).start()
        Send(got.at[rows], got_r.at[rows], f_s.at[1], f_r.at[1], -1, 0).start()
    onward = [
        Send(got, got_l, f_s.at[0], f_r.at[0], 1, 0),
        Send(got, got_r, f_s.at[1], f_r.at[1], -1, 0),
    ]
    late += onward

    def add_loads(ref, first, x_local):
        lane = lax.broadcasted_iota(jnp.int32, (64, 128), 1)
        source = lax.broadcasted_iota(jnp.int32, (64, 128), 0)
        key = jnp.zeros((1, 128), F32)
        for k in range(2):
            rows = ref[pl.ds(4 * k + 3, 64, stride=8), :]
            key = key + jnp.sum(jnp.where(lane == source + 64 * k, rows, 0.0), axis=0, keepdims=True)
        flat = jnp.concatenate(
            [
                jnp.concatenate([ref[pl.ds(4 * k + c, 64, stride=8), :] for k in range(2)], axis=0)
                for c in range(3)
            ],
            axis=1,
        )
        values = jnp.concatenate(halves(flat), axis=0)
        shape = (4, TF, 8, 128)
        row = s * 32 - 8 + lax.broadcasted_iota(jnp.int32, shape, 2) * TF + lax.broadcasted_iota(jnp.int32, shape, 1)
        for part in range(2):
            cell = lax.broadcasted_iota(jnp.int32, shape, 0) + (x_local + 4 * part)
            cell = jnp.where((row >= 0) & (row < 32 * SEC), cell * 128 + row + 1, -1)
            hit = (cell.astype(F32) == key.reshape(1, 1, 1, 128)).astype(F32)
            hit = hit.reshape(4 * TF * 8, 128).astype(BF16)
            loads = jnp.dot(jnp.concatenate([hit, hit], axis=1), values, preferred_element_type=F32)
            at = first + 4 * part
            for c in range(3):
                load = loads[:, 128 * c : 128 * c + 128].reshape(shape)
                ff[c, pl.ds(at, 4)] += load
                load = ra0[pl.ds(at, 4)] * load
                aa[c, pl.ds(at, 4)] += load
                wb[c, pl.ds(at, 4)] += load

    def defect_one(lo, hi):
        def step(x, count):
            for c in range(3):
                at = pl.ds(2 * x, 2 * count)
                w, n = around(wa, c, 2 * x, 2 * count, 1.0)
                d = (ff[c, at] - e0[at] * w) + q0[at] * n
                for i in range(count):
                    pair = d[2 * i] + d[2 * i + 1]
                    for j in range(T1):
                        here = pair[2 * j] + pair[2 * j + 1]
                        d1[c, x + i, j] = here
                        a1[c, x + i, j] = ra1[x + i, j] * here

        over(lo, hi, 1, step)

    add_loads(got, 8, 0)
    add_loads(got, 16, 8)
    fine_sweep(wb, wa, 10, 22)
    defect_one(6, 10)

    arrive(mat_len + mat_corners)
    for lo, hi in ((0, 8), (24, 32)):
        lax.fori_loop(lo, hi, fine_coefficients, 0)
        lax.fori_loop(lo // 2, hi // 2, one_coefficients, 0)
    for lo, hi in ((0, 2), (6, 8)):
        lax.fori_loop(lo, hi, two_coefficients, 0)
    arrive(pred_len + pred_corners)
    for lo, hi in ((0, 8), (24, 32)):
        lax.fori_loop(lo, hi, start_fine, 0)
    fine_sweep(wa, wb, 2, 9)
    fine_sweep(wa, wb, 23, 30)
    onward[0].came()
    add_loads(got_l, 0, 8)
    onward[1].came()
    add_loads(got_r, 24, 0)
    fine_sweep(wb, wa, 3, 10)
    fine_sweep(wb, wa, 22, 29)
    defect_one(2, 6)
    defect_one(10, 14)

    def first_correction(x, count):
        at = pl.ds(x, count)
        for c in range(3):
            w, n = around(a1, c, x, count, 4.0)
            wc[c, at] = 1.3 * w + b1[at] * n

    over(3, 13, 5, first_correction)

    def keep_own(x, _):
        for c in range(3):
            for k, ref in enumerate((a1, wc)):
                for j in range(T1):
                    pn[2 * c + k, pl.ds(j, 8, stride=T1), :] = ref[c, x, j]
                nat[k, c, x, 4:20, :] = pn[2 * c + k, 4:20, :]
        return 0

    for c in range(3):
        w, n = around(wc, c, 4, 8, 4.0)
        d = (d1[c, 4:12] - e1[4:12] * w) + q1[4:12] * n
        for x2 in range(4):
            pair = d[2 * x2] + d[2 * x2 + 1]
            deft[c, x2] = own_rows_of_pairs(4 * c + x2, [pair[j] for j in range(T1)])

    came()
    whole_z = jnp.ones((8, 128), F32)
    f = [fac2[x] for x in range(X2)]

    def chain(off):
        total = off[0]
        for x in range(1, 4):
            total = off[x] + f[2 + x] * total
        return total

    def carried_in(ref_y, came_y, ref_z, i):
        came_y()

        def join(k, total):
            return tuple(ref_y[k, c] + slope_y[k] * total[c] for c in range(3))

        zero = tuple(jnp.zeros((8, 128), F32) for _ in range(3))
        mine = lax.fori_loop(0, r, join, zero)
        whole = lax.fori_loop(r, 8, join, mine)
        came_z, gone_z = gather_z(ref_z, jnp.stack(whole), i)

        def finish():
            came_z()

            def join_z(k, total):
                return tuple(ref_z[k, c] + slope_z[k] * total[c] for c in range(3))

            before = lax.fori_loop(0, z, join_z, zero)
            return [mine[c] + ahead * before[c] for c in range(3)]

        return finish, gone_z

    off = [[rq2[2 + x] * deft[c, x] for x in range(4)] for c in range(3)]
    came, gone_y1 = gather_y(g1, jnp.stack([chain(off[c]) for c in range(3)]), 1)
    for c in range(3):
        s_first[c] = off[c][0]
    first = Send(s_first, r_first, n_s.at[0], n_r.at[0], -1, 0)
    first.start()
    late.append(first)

    lax.fori_loop(4, 12, keep_own, 0)
    nat_up = Send(nat.at[:, :, 4:12, 16:20, :], nat.at[:, :, 4:12, 0:4, :], x_s.at[0], x_r.at[0], 0, 1)
    nat_dn = Send(nat.at[:, :, 4:12, 4:8, :], nat.at[:, :, 4:12, 20:24, :], x_s.at[1], x_r.at[1], 0, -1)
    nat_up.start()
    nat_dn.start()
    late += [nat_up, nat_dn]

    finish, gone_z1 = carried_in(g1, came, z1, 1)
    nat_up.came()
    nat_dn.came()
    nat_right = Send(nat.at[:, :, 8:12], nat.at[:, :, 0:4], x_s.at[2], x_r.at[2], 1, 0)
    nat_left = Send(nat.at[:, :, 4:8], nat.at[:, :, 12:16], x_s.at[3], x_r.at[3], -1, 0)
    nat_right.start()
    nat_left.start()
    late += [nat_right, nat_left]
    first.came()
    carry = finish()

    w1 = []
    for c in range(3):
        line = []
        at = carry[c]
        for x in range(4):
            at = off[c][x] + f[2 + x] * at
            line.append(at)
        line.append(r_first[c] + f[6] * at)
        w1.append(line)
    for i in range(12):
        w1s[8 * i : 8 * i + 8, :] = w1[i // 4][i % 4]
    w1s[96:128, :] = jnp.zeros((32, 128), F32)
    up_s[...] = w1s[pl.ds(7, 16, stride=8), :]
    dn_s[...] = w1s[pl.ds(0, 16, stride=8), :]
    rows_up = Send(up_s, up_r, n_s.at[1], n_r.at[1], 0, 1)
    rows_dn = Send(dn_s, dn_r, n_s.at[2], n_r.at[2], 0, -1)
    rows_up.start()
    rows_dn.start()
    late += [rows_up, rows_dn]
    depth = [[16.0 * shift_depth(w1[c][x]) for x in range(4)] for c in range(3)]
    rows_up.came()
    rows_dn.came()
    off = []
    for c in range(3):
        line = []
        for x in range(4):
            i = 4 * c + x
            w = w1[c][x]
            below = jnp.where(sub == 0, up_r[i : i + 1, :], pltpu.roll(w, 1, 0))
            above = jnp.where(sub == 7, dn_r[i : i + 1, :], pltpu.roll(w, 7, 0))
            n = 12.0 * w1[c][x + 1] + ((below + above) + depth[c][x])
            line.append(rq2[2 + x] * (deft[c, x] + q2[2 + x] * n))
        off.append(line)

    came, gone_y2 = gather_y(g2, jnp.stack([chain(off[c]) for c in range(3)]), 2)
    for c in range(3):
        s_ends[c, 0] = off[c][0]
        s_ends[c, 1] = off[c][1]
        s_ends[c, 2] = off[c][3]
    to_left = Send(s_ends.at[:, 0:2], r_right, n_s.at[3], n_r.at[3], -1, 0)
    to_right = Send(s_ends.at[:, 2:3], r_left, n_s.at[4], n_r.at[4], 1, 0)
    to_left.start()
    to_right.start()
    late += [to_left, to_right]
    finish, gone_z2 = carried_in(g2, came, z2, 2)
    to_left.came()
    to_right.came()
    nat_right.came()
    nat_left.came()
    carry = finish()

    back = jnp.where(l > 0, 1.0, 0.0) / jnp.where(l > 0, f[1], 1.0)
    for c in range(3):
        line = [(carry[c] - r_left[c, 0]) * back, carry[c]]
        at = carry[c]
        for x in range(6):
            shift = off[c][x] if x < 4 else r_right[c, x - 4]
            at = shift + f[2 + x] * at
            line.append(at)
        for x in range(X2):
            i = 8 * (c * X2 + x)
            v2s[i : i + 8, :] = iq2[x] * line[x]
    for k in range(2):
        va_s[24 * k : 24 * k + 24, :] = v2s[pl.ds(6 + k, 24, stride=8), :]
        vb_s[24 * k : 24 * k + 24, :] = v2s[pl.ds(k, 24, stride=8), :]
    ends_up = Send(va_s, va_r, n_s.at[5], n_r.at[5], 0, 1)
    ends_dn = Send(vb_s, vb_r, n_s.at[6], n_r.at[6], 0, -1)
    ends_up.start()
    ends_dn.start()
    late += [ends_up, ends_dn]

    for i in range(24):
        v = v2s[8 * i : 8 * i + 8, :]
        pn[i, pl.ds(4, 8, stride=2), :] = v
        pn[i, pl.ds(5, 8, stride=2), :] = v
    ends_up.came()
    ends_dn.came()
    for i in range(24):
        for k in range(2):
            pn[i, 2 * k : 2 * k + 2, :] = jnp.broadcast_to(va_r[24 * k + i : 24 * k + i + 1, :], (2, 128))
            pn[i, 20 + 2 * k : 22 + 2 * k, :] = jnp.broadcast_to(vb_r[24 * k + i : 24 * k + i + 1, :], (2, 128))

    def correct_one(x2, _):
        for c in range(3):
            for j in range(T1):
                v = pn[c * X2 + x2, pl.ds(j, 8, stride=T1), :]
                for i in range(2):
                    x = 2 * x2 + i
                    a1[c, x, j] = nat[0, c, x, pl.ds(j, 8, stride=T1), :]
                    wc[c, x, j] = nat[1, c, x, pl.ds(j, 8, stride=T1), :] + q1[x, j] * v
        return 0

    lax.fori_loop(0, X2, correct_one, 0)

    def one_sweep(src, dst, lo, hi):
        def step(x, count):
            at = pl.ds(x, count)
            for c in range(3):
                w, n = around(src, c, x, count, 4.0)
                dst[c, at] = (0.3 * w + a1[c, at]) + b1[at] * n

        over(lo, hi, ONE_GROUP, step)

    one_sweep(wc, wd, 1, 15)
    one_sweep(wd, wc, 2, 14)

    def correct_fine(x, _):
        for c in range(3):
            v = iq1[x] * wc[c, x]
            for i in range(2):
                for j in range(TF):
                    at = 2 * x + i
                    wb[c, at, j] = wa[c, at, j] + q0[at, j] * v[j // 2]
        return 0

    lax.fori_loop(2, 14, correct_fine, 0)
    fine_sweep(wb, wa, 5, 27)
    fine_sweep(wa, wb, 6, 26)

    def results(x, count):
        at = pl.ds(x, count)
        for c in range(3):
            w, n = around(wb, c, x, count, 1.0)
            value = iq0[at] * w
            rest = (ff[c, at] - e0[at] * w) + q0[at] * n
            for i in range(count):
                for j in range(TF):
                    on_v[c, x - 8 + i, pl.ds(j, 8, stride=TF), :] = value[i, j]
                    on_r[c, x - 8 + i, pl.ds(j, 8, stride=TF), :] = rest[i, j]

    outs = []
    for half in range(2):
        over(8 + 8 * half, 16 + 8 * half, 2, results)
        rows = slice(8 * half, 8 * half + 8)
        for k, (src, dst) in enumerate(((on_v, out_v), (on_r, out_r))):
            copy = pltpu.make_async_copy(src.at[:, rows, 8:40, :], dst.at[:, rows], o_s.at[2 * half + k])
            copy.start()
            outs.append(copy)
    remote(sent.at[0:504], got.at[0:504], a_s.at[0], a_r.at[0], there(0, 0)).wait_send()
    for h in late:
        h.sent()
    for gone in (gone_y0, gone_z0, gone_y1, gone_z1, gone_y2, gone_z2):
        gone()
    for copy in outs:
        copy.wait()


def shards(predicted, material, stiffness, density, tile, row, force):
    anywhere = pl.BlockSpec(memory_space=pl.ANY)
    vmem = pl.BlockSpec(memory_space=pltpu.VMEM)
    smem = pl.BlockSpec(memory_space=pltpu.SMEM)

    def v(*shape, dtype=F32):
        return pltpu.VMEM(shape, dtype)

    dma = pltpu.SemaphoreType.DMA
    scratch = [
        v(3, XE, 48, 128), v(XE, 48, 128, dtype=jnp.int32),
        v(512, 128), v(512, 128), v(512, 128), v(512, 128),
        *[v(XE, TF, 8, 128) for _ in range(6)],
        *[v(3, XE, TF, 8, 128) for _ in range(4)],
        *[v(X1, T1, 8, 128) for _ in range(6)],
        *[v(3, X1, T1, 8, 128) for _ in range(4)],
        v(2, 3, X1, 24, 128), v(3, 4, 8, 128),
        *[v(X2, 8, 128) for _ in range(4)],
        v(8, 8, 128), v(8, 8, 128),
        *[v(8, 3, 8, 128) for _ in range(4)],
        v(3, 8, 128), v(3, 8, 128), v(3, 3, 8, 128), v(3, 2, 8, 128), v(3, 1, 8, 128),
        v(128, 128), *[v(16, 128) for _ in range(4)],
        v(192, 128), *[v(48, 128) for _ in range(4)],
        v(24, 24, 128), v(3, 16, 48, 128), v(3, 16, 48, 128),
        dma((2,)), dma((16,)), dma((16,)), dma((1,)), dma((8,)), dma((2,)), dma((2,)),
        dma((3, 8)), dma((3, 8)), dma((3, 8)), dma((3, 8)),
        dma((7,)), dma((7,)), dma((4,)), dma((4,)), dma((4,)),
    ]
    result = jax.ShapeDtypeStruct(predicted.shape, F32)
    return pl.pallas_call(
        body,
        out_shape=(result, result),
        in_specs=[pl.BlockSpec(memory_space=pltpu.HBM), pl.BlockSpec(memory_space=pltpu.HBM), smem, smem, vmem, vmem, vmem],
        out_specs=(anywhere, anywhere),
        scratch_shapes=scratch,
        compiler_params=pltpu.CompilerParams(
            collective_id=0, has_side_effects=True, vmem_limit_bytes=48 * 2**20
        ),
    )(
        predicted, material, stiffness, density,
        tile.reshape(1, -1), row.reshape(1, -1), jnp.transpose(force, (1, 0, 2)),
    )


def solution(mesh):
    placed = (
        P(None, "len", "sec", None),
        P("len", "sec", None),
        P(),
        P(),
        P("len", None),
        P("len"),
        P("len", None, None),
    )
    return jax.shard_map(
        shards,
        mesh=mesh,
        in_specs=placed,
        out_specs=(P(None, "len", "sec", None), P(None, "len", "sec", None)),
        check_vma=False,
    )
```
